128 devices in a mesh: shard: 8 (over x, core), split: 16 (over z, y).
Axes of the slice: x: 4, y: 4, z: 4, core: 2. Of those that a mesh axis runs over, the one named last changes fastest.
Arguments:
- embedding: bfloat16 [65536, 512], P(('shard', 'split')), may hold values from -200 to 200
- cluster: int32 [65536], P(('shard', 'split')), may hold values from 0 to 31, as said below
- rank: int32 [65536], P(('shard', 'split')), may hold values from 0 to 1048575
Outputs:
- best_similarity: float32 [65536], P(('shard', 'split'))
The draws below stay inside these ranges and needn't reach their ends.
Inputs may be any that keep to these rules, and one draw needn't show every extreme that they name: The rows of one device hold at most 32 rows of any one cluster, and exactly 32 rows of some cluster.
All inputs are finite; a program needn't handle non-finite values.
Results may differ from the reference program's by a relative error of at most 0.00055.
Values may be sent and summed in bfloat16 or wider, within the bound.
A program may use at most 64 MiB of HBM per device.

```python
import jax
import jax.numpy as jnp
from jax import lax

D = 512
ROWS_DEV = 512
PROTOS = 256
RANK_LIMIT = 1048576
NCLUST = 32
MOST = 32
ROWS = 65536
DEVICES = 128


def shared_labels(key):
    k_count, k_star, k_noise, k_family = jax.random.split(key, 4)
    quota = jax.random.randint(k_count, (NCLUST,), MOST // 2, MOST + 1)
    star = jax.random.randint(k_star, (DEVICES,), 0, NCLUST)
    pool = jnp.arange(NCLUST * MOST, dtype=jnp.int32) // MOST
    within = jnp.arange(NCLUST * MOST, dtype=jnp.int32) % MOST

    def one_block(star_one, key_one):
        key_a, key_b = jax.random.split(key_one)
        noise = jax.random.permutation(key_a, NCLUST * MOST).astype(jnp.int32)
        quota_here = jnp.where(jnp.arange(NCLUST) == star_one, MOST, quota)
        eligible = within < quota_here[pool]
        score = jnp.where(pool == star_one, within, jnp.where(eligible, MOST + noise, MOST + NCLUST * MOST + noise))
        chosen = pool[jnp.argsort(score)[:ROWS_DEV]]
        return chosen[jax.random.permutation(key_b, ROWS_DEV)]
    labels = jax.vmap(one_block)(star, jax.random.split(k_noise, DEVICES)).reshape(ROWS)
    family = jax.random.randint(k_family, (ROWS,), 0, PROTOS)
    return (labels.astype(jnp.int32), family.astype(jnp.int32))


def draw_cluster(key, part):
    labels, family = shared_labels(key)
    return labels


def draw_embedding(key, part):
    labels, family = shared_labels(key)
    key = jax.random.fold_in(key, 7)
    k_table, k_weight, k_noise = jax.random.split(key, 3)
    table = jax.random.normal(k_table, (NCLUST * PROTOS, D), jnp.float32)
    weight = jax.random.uniform(k_weight, (ROWS, 1), jnp.float32, 0.2, 2.0)
    source = weight * table[labels * PROTOS + family]
    noise = jax.random.normal(k_noise, (ROWS, D), jnp.float32)
    values = source + noise
    return values.astype(jnp.bfloat16)


def plant(values, rng, low, high):
    dims = values.shape
    spot = [jax.random.randint(jax.random.fold_in(rng, axis), (), 0, dims[axis]) for axis in range(len(dims))]
    values = values.at[tuple(spot)].set(low)
    longest = dims.index(max(dims))
    spot[longest] = (spot[longest] + 1) % dims[longest]
    return values.at[tuple(spot)].set(high)


def setup_inputs(seed: int = 0) -> dict:
    splits = jax.random.split(jax.random.key(seed), 4)
    return {
        "embedding": draw_embedding(jax.random.fold_in(splits[3], 71), 0),
        "cluster": draw_cluster(jax.random.fold_in(splits[3], 71), 0),
        "rank": plant(jax.random.randint(splits[2], (ROWS,), 0, RANK_LIMIT), jax.random.fold_in(splits[2], 1), 0, RANK_LIMIT - 1).astype(jnp.int32),
    }


def reference(embedding, cluster, rank):
    values32 = embedding.astype(jnp.float32)
    unit = (values32 * lax.rsqrt(lax.optimization_barrier(jnp.sum(values32 * values32, axis=1, keepdims=True)) + 1e-06)).astype(jnp.bfloat16)
    order = jnp.argsort(cluster, stable=True).astype(jnp.int32)
    onehot = (cluster[:, None] == jnp.arange(NCLUST, dtype=jnp.int32)[None, :]).astype(jnp.int32)
    counts = lax.optimization_barrier(jnp.sum(onehot, axis=0)).astype(jnp.int32)
    starts = (jnp.cumsum(counts) - counts).astype(jnp.int32)
    capacity = DEVICES * MOST
    order_padded = jnp.concatenate([order, jnp.zeros((capacity,), jnp.int32)])

    def one_cluster(label):
        members_idx = lax.dynamic_slice_in_dim(order_padded, starts[label].astype(jnp.int32), capacity)
        valid = jnp.arange(capacity, dtype=jnp.int32) < counts[label]
        members = unit[members_idx]
        member_rank = jnp.where(valid, rank[members_idx], jnp.int32(1 << 30))
        scores = jnp.dot(members, members.T, preferred_element_type=jnp.float32)
        allowed = member_rank[None, :] < member_rank[:, None]
        found = lax.optimization_barrier(jnp.max(jnp.where(allowed, scores, jnp.float32(-1.0)), axis=1))
        return (jnp.where(valid, members_idx, jnp.int32(ROWS)), found)
    places, found_all = lax.map(one_cluster, jnp.arange(NCLUST, dtype=jnp.int32))
    result = jnp.full((ROWS,), -1.0, jnp.float32)
    return result.at[places.reshape(-1)].set(found_all.reshape(-1), mode='drop')
```

```python
import jax
import jax.numpy as jnp
from jax import lax
from jax.experimental import pallas as pl
from jax.experimental.pallas import tpu as pltpu
from jax.sharding import PartitionSpec as P

MESH = pl.DeviceIdType.MESH
CLUSTERS = 32
SLOTS = 32
CHIPS = 64
BLOCK = 256
BLOCKS = 8
NO_RANK = float(1 << 30)


def place(x, y, z, core):
    return (2 * x + core, 4 * z + y)


def kernel(
    embedding_ref, cluster_ref, rank_ref, out_ref,
    outgoing, out_rank, members, member_rank, rank_column, rank_row, best, back,
    send_sem, rank_send_sem, member_sem, rank_sem, pair_send_sem, pair_rank_send_sem, pair_sem, pair_rank_sem,
    back_send_sem, back_sem,
):
    shard, split = lax.axis_index("shard"), lax.axis_index("split")
    x, core, z, y = shard // 2, shard % 2, split // 4, split % 4
    chip = x + 4 * y + 16 * z
    group = chip // 4
    holds = (x + y + z) % 2 == 0
    own = x + 4 * y + 16 * (z // 2)
    rows = embedding_ref.shape[0]

    barrier = pltpu.get_barrier_semaphore()

    @pl.when(holds)
    def _():
        def greet(s, carry):
            pl.semaphore_signal(
                barrier, inc=1, device_id=place(s % 4, (s // 4) % 4, s // 16, core), device_id_type=MESH
            )
            return carry

        lax.fori_loop(0, CHIPS, greet, 0)
        pl.semaphore_signal(barrier, inc=1, device_id=place(x, y, z, 1 - core), device_id_type=MESH)

    values = embedding_ref[...].astype(jnp.float32)
    unit = (
        values * lax.rsqrt(jnp.sum(values * values, axis=1, keepdims=True) + 1e-06)
    ).astype(jnp.bfloat16)
    cluster = cluster_ref[...]
    rank = rank_ref[...]
    cluster_hit = lax.broadcasted_iota(jnp.int32, (CLUSTERS, rows), 0) == cluster
    onehot = cluster_hit.astype(jnp.float32)
    earlier = (
        lax.broadcasted_iota(jnp.int32, (rows, rows), 0) < lax.broadcasted_iota(jnp.int32, (rows, rows), 1)
    ).astype(jnp.float32).astype(jnp.bfloat16)
    before = jnp.dot(onehot.astype(jnp.bfloat16), earlier, preferred_element_type=jnp.float32)
    position = jnp.sum(before * onehot, axis=0, keepdims=True).astype(jnp.int32)
    slot = cluster * SLOTS + position

    def fill(part, carry):
        base = part * 256
        pick = (lax.broadcasted_iota(jnp.int32, (256, rows), 0) + base == slot).astype(jnp.float32).astype(jnp.bfloat16)
        packed = jnp.dot(pick, unit, preferred_element_type=jnp.float32).astype(jnp.bfloat16)
        outgoing[pl.ds(part * 8, 8)] = packed.reshape(8, SLOTS, packed.shape[1])
        return carry

    lax.fori_loop(0, CLUSTERS * SLOTS // 256, fill, 0)

    lane = lax.broadcasted_iota(jnp.int32, (128, rows), 0)
    lane_hit = (lane == position + SLOTS * x).astype(jnp.float32).astype(jnp.bfloat16)
    contract_last = (((1,), (1,)), ((), ()))

    def spread(part):
        return lax.dot_general(
            (onehot * part.astype(jnp.float32)).astype(jnp.bfloat16), lane_hit, contract_last,
            preferred_element_type=jnp.float32,
        )

    taken = spread(jnp.ones_like(rank))
    slot_rank = (
        spread(rank % 128) + 128.0 * spread(rank // 128 % 128) + 16384.0 * spread(rank // 16384)
    )
    mine = lax.broadcasted_iota(jnp.int32, (CLUSTERS, 128), 1) // SLOTS == x
    out_rank[...] = jnp.where(mine, jnp.where(taken > 0.5, slot_rank, NO_RANK), 0.0).reshape(CLUSTERS, 1, 128)

    pl.semaphore_wait(barrier, CLUSTERS + jnp.where(holds, 1, 0))

    block = chip // 8
    slot_in_block = chip % 8

    def send(t, carry):
        c = (t + chip // 2) % CLUSTERS
        cx, cy = c % 4, (c // 4) % 4
        cz = 2 * (c // 16) + (cx + cy) % 2
        here = (cx == x) & (cy == y) & (cz == z)

        @pl.when(jnp.logical_not(here))
        def _():
            pltpu.make_async_remote_copy(
                out_rank.at[c], member_rank.at[0, block, slot_in_block], rank_send_sem, rank_sem.at[block],
                device_id=place(cx, cy, cz, core), device_id_type=MESH,
            ).start()
            pltpu.make_async_remote_copy(
                outgoing.at[c], members.at[0, block, pl.ds(pl.multiple_of(slot_in_block * SLOTS, SLOTS), SLOTS)],
                send_sem, member_sem.at[block], device_id=place(cx, cy, cz, core), device_id_type=MESH,
            ).start()

        @pl.when(here)
        def _():
            pltpu.make_async_copy(
                out_rank.at[c], member_rank.at[0, block, slot_in_block], rank_sem.at[block]
            ).start()
            pltpu.make_async_copy(
                outgoing.at[c], members.at[0, block, pl.ds(pl.multiple_of(slot_in_block * SLOTS, SLOTS), SLOTS)],
                member_sem.at[block],
            ).start()

        return carry

    lax.fori_loop(0, CLUSTERS, send, 0)

    def arrived(ref, sem):
        pltpu.make_async_copy(ref, ref, sem).wait()

    @pl.when(holds)
    def _():
        best[...] = jnp.full(best.shape, -1.0, jnp.float32)

        def tile(side, j, i):
            scores = lax.dot_general(
                members[side, j], members[0, i], contract_last, preferred_element_type=jnp.float32
            )
            lower = jnp.concatenate([rank_column[side, j], rank_column[side, j]], axis=1) < rank_row[i]
            found = jnp.where(lower, scores, -1.0).reshape(BLOCK // 8, 8, BLOCK)
            best[i] = jnp.maximum(best[i], jnp.max(found, axis=0))

        def ranks(side, b):
            eight = member_rank[side, b].reshape(8, 128)
            halves = [jnp.sum(eight[4 * h : 4 * h + 4], axis=0, keepdims=True) for h in range(2)]
            if side == 0:
                rank_row[b] = jnp.concatenate(halves, axis=1)
            for h in range(2):
                rank_column[side, b, pl.ds(128 * h, 128)] = jnp.broadcast_to(halves[h], (128, 128)).T

        def step(b, carry):
            arrived(member_rank.at[0, b], rank_sem.at[b])
            arrived(members.at[0, b], member_sem.at[b])
            sibling = place(x, y, z, 1 - core)
            pltpu.make_async_remote_copy(
                member_rank.at[0, b], member_rank.at[1, b], pair_rank_send_sem, pair_rank_sem.at[b],
                device_id=sibling, device_id_type=MESH,
            ).start()
            pltpu.make_async_remote_copy(
                members.at[0, b], members.at[1, b], pair_send_sem, pair_sem.at[b],
                device_id=sibling, device_id_type=MESH,
            ).start()
            ranks(0, b)
            lax.fori_loop(0, b + 1, lambda j, c: (tile(0, j, b), c)[1], 0)
            lax.fori_loop(0, b, lambda i, c: (tile(0, b, i), c)[1], 0)
            arrived(member_rank.at[1, b], pair_rank_sem.at[b])
            arrived(members.at[1, b], pair_sem.at[b])
            ranks(1, b)
            lax.fori_loop(0, b + 1, lambda j, c: (tile(1, j, b), c)[1], 0)
            lax.fori_loop(0, b, lambda i, c: (tile(1, b, i), c)[1], 0)
            return carry

        lax.fori_loop(0, BLOCKS, step, 0)

        def reply(s, carry):
            sx, sy, sz = s % 4, (s // 4) % 4, s // 16
            here = s == chip
            lanes = pl.ds(pl.multiple_of(sy % 2 * 128, 128), 128)

            @pl.when(jnp.logical_not(here))
            def _():
                pltpu.make_async_remote_copy(
                    best.at[s // 8, :, lanes], back.at[own], back_send_sem, back_sem,
                    device_id=place(sx, sy, sz, core), device_id_type=MESH,
                ).start()

            @pl.when(here)
            def _():
                pltpu.make_async_copy(best.at[s // 8, :, lanes], back.at[own], back_sem).start()

            return carry

        lax.fori_loop(0, CHIPS, reply, 0)

    arrived(back, back_sem)
    table = jnp.max(back[...], axis=1)
    column = lax.broadcasted_iota(jnp.int32, (128, rows), 0) == position + SLOTS * x
    found = lax.dot_general(
        table, onehot, (((0,), (0,)), ((), ())),
        precision=lax.Precision.HIGHEST, preferred_element_type=jnp.float32,
    )
    out_ref[...] = jnp.sum(jnp.where(column, found, 0.0), axis=0, keepdims=True)

    @pl.when(holds)
    def _():
        arrived(outgoing.at[pl.ds(0, CLUSTERS - 1)], send_sem)
        arrived(out_rank.at[pl.ds(0, CLUSTERS - 1)], rank_send_sem)
        arrived(members.at[0], pair_send_sem)
        arrived(member_rank.at[0], pair_rank_send_sem)
        arrived(back, back_send_sem)
        arrived(back.at[pl.ds(0, CLUSTERS - 1)], back_send_sem)

    @pl.when(jnp.logical_not(holds))
    def _():
        arrived(outgoing, send_sem)
        arrived(out_rank, rank_send_sem)


def body(embedding, cluster, rank):
    rows, width = embedding.shape
    vmem = pl.BlockSpec(memory_space=pltpu.VMEM)
    dma = pltpu.SemaphoreType.DMA
    found = pl.pallas_call(
        kernel,
        out_shape=jax.ShapeDtypeStruct((1, rows), jnp.float32),
        in_specs=[vmem] * 3,
        out_specs=vmem,
        scratch_shapes=[
            pltpu.VMEM((CLUSTERS, SLOTS, width), jnp.bfloat16),
            pltpu.VMEM((CLUSTERS, 1, 128), jnp.float32),
            pltpu.VMEM((2, BLOCKS, BLOCK, width), jnp.bfloat16),
            pltpu.VMEM((2, BLOCKS, 8, 1, 128), jnp.float32),
            pltpu.VMEM((2, BLOCKS, BLOCK, 128), jnp.float32),
            pltpu.VMEM((BLOCKS, 1, BLOCK), jnp.float32),
            pltpu.VMEM((BLOCKS, 8, BLOCK), jnp.float32),
            pltpu.VMEM((CLUSTERS, 8, 128), jnp.float32),
            dma, dma, dma((BLOCKS,)), dma((BLOCKS,)), dma, dma, dma((BLOCKS,)), dma((BLOCKS,)), dma, dma,
        ],
        compiler_params=pltpu.CompilerParams(
            collective_id=0, has_side_effects=True, vmem_limit_bytes=48 << 20
        ),
    )(embedding, cluster.reshape(1, rows), rank.reshape(1, rows))
    return found.reshape(rows)


def solution(mesh):
    return jax.shard_map(
        body,
        mesh=mesh,
        in_specs=(P(("shard", "split"), None), P(("shard", "split")), P(("shard", "split"))),
        out_specs=P(("shard", "split")),
        check_vma=False,
    )
```

```python
import jax
import jax.numpy as jnp
from jax import lax
from jax.experimental import pallas as pl
from jax.experimental.pallas import tpu as pltpu
from jax.sharding import PartitionSpec as P

MESH = pl.DeviceIdType.MESH
CLUSTERS = 32
SLOTS = 32
GROUP = 4 * SLOTS
GROUPS = 16
PARITY = 1
NO_RANK = float(1 << 30)
ORDER = [
    (1, 2), (3, 2), (2, 2), (0, 2), (2, 1), (2, 3), (1, 1), (3, 3),
    (3, 1), (1, 3), (0, 1), (0, 3), (2, 0), (1, 0), (3, 0), (0, 0),
]
RELAYED = [(1, 2), (3, 2)]
STEPS = [4, 4, 4, 2, 1, 1]
STARTS = [sum(STEPS[:k]) for k in range(len(STEPS) + 1)]


def place(x, y, z, core):
    return (2 * x + core, 4 * z + y)


def step_of(t):
    return max(k for k in range(len(STEPS)) if STARTS[k] <= t)


def arrived(ref, sem):
    pltpu.make_async_copy(ref, ref, sem).wait()


def remote(src, dst, send_sem, recv_sem, target):
    return pltpu.make_async_remote_copy(
        src, dst, send_sem, recv_sem, device_id=target, device_id_type=MESH
    )


def kernel(
    embedding_ref, cluster_ref, rank_ref, out_ref,
    outgoing, out_rank, passing, passing_rank, members, member_rank, rank_column, rank_row, best, back,
    send_sem, rank_send_sem, pass_sem, pass_rank_sem, pass_send_sem, pass_rank_send_sem, member_sem, rank_sem,
    pair_send_sem, pair_rank_send_sem, pair_sem, pair_rank_sem, back_send_sem, back_sem,
):
    shard, split = lax.axis_index("shard"), lax.axis_index("split")
    x, core, z, y = shard // 2, shard % 2, split // 4, split % 4
    holds = (x + y + z) % 2 == PARITY
    own = x + 4 * y + 16 * (z // 2)
    rows = embedding_ref.shape[0]

    barrier = pltpu.get_barrier_semaphore()

    def greet(gx, gy, gz, gcore):
        pl.semaphore_signal(barrier, inc=1, device_id=place(gx, gy, gz, gcore), device_id_type=MESH)

    @pl.when(holds)
    def _():
        def each(s, carry):
            greet(s % 4, (s // 4) % 4, s // 16, core)
            return carry

        lax.fori_loop(0, 64, each, 0)
        greet(x, y, z, 1 - core)

    @pl.when(jnp.logical_not(holds))
    def _():
        for sy in range(4):
            greet(x, sy, (z + 2) % 4, core)

    values = embedding_ref[...].astype(jnp.float32)
    unit = (
        values * lax.rsqrt(jnp.sum(values * values, axis=1, keepdims=True) + 1e-06)
    ).astype(jnp.bfloat16)
    cluster = cluster_ref[...]
    rank = rank_ref[...]
    cluster_hit = lax.broadcasted_iota(jnp.int32, (CLUSTERS, rows), 0) == cluster
    onehot = cluster_hit.astype(jnp.float32)
    earlier = (
        lax.broadcasted_iota(jnp.int32, (rows, rows), 0) < lax.broadcasted_iota(jnp.int32, (rows, rows), 1)
    ).astype(jnp.float32).astype(jnp.bfloat16)
    before = jnp.dot(onehot.astype(jnp.bfloat16), earlier, preferred_element_type=jnp.float32)
    position = jnp.sum(before * onehot, axis=0, keepdims=True).astype(jnp.int32)
    slot = cluster * SLOTS + position

    def fill(part, carry):
        pick = (
            lax.broadcasted_iota(jnp.int32, (256, rows), 0) + part * 256 == slot
        ).astype(jnp.float32).astype(jnp.bfloat16)
        packed = jnp.dot(pick, unit, preferred_element_type=jnp.float32).astype(jnp.bfloat16)
        outgoing[pl.ds(part * 8, 8)] = packed.reshape(8, SLOTS, packed.shape[1])
        return carry

    lax.fori_loop(0, CLUSTERS * SLOTS // 256, fill, 0)

    lane_hit = lax.broadcasted_iota(jnp.int32, (GROUP, rows), 0) == position + SLOTS * y
    lane_onehot = lane_hit.astype(jnp.float32).astype(jnp.bfloat16)
    contract_last = (((1,), (1,)), ((), ()))

    def spread(part):
        return lax.dot_general(
            (onehot * part.astype(jnp.float32)).astype(jnp.bfloat16), lane_onehot, contract_last,
            preferred_element_type=jnp.float32,
        )

    taken = spread(jnp.ones_like(rank))
    slot_rank = (
        spread(rank % 128) + 128.0 * spread(rank // 128 % 128) + 16384.0 * spread(rank // 16384)
    )
    mine = lax.broadcasted_iota(jnp.int32, (CLUSTERS, GROUP), 1) // SLOTS == y
    out_rank[...] = jnp.where(mine, jnp.where(taken > 0.5, slot_rank, NO_RANK), 0.0).reshape(CLUSTERS, 1, GROUP)

    pl.semaphore_wait(barrier, CLUSTERS + 2 + jnp.where(holds, 1, 0))

    for t, (dx, dz) in enumerate(ORDER):
        ax, az = (x + 4 - dx) % 4, (z + 4 - dz) % 4
        for half in range(2):
            ay = (y + (ax + y + az + PARITY) % 2 + 2 * half) % 4
            c = ax + 4 * ay + 16 * (az // 2)
            if (dx, dz) in RELAYED:
                side = RELAYED.index((dx, dz))
                target = place(x, ay, az, core)
                remote(
                    out_rank.at[c], passing_rank.at[side, y], rank_send_sem, pass_rank_sem.at[side], target
                ).start()
                remote(outgoing.at[c], passing.at[side, y], send_sem, pass_sem.at[side], target).start()
                continue
            k = step_of(t)
            rank_there, rank_there_sem = member_rank.at[0, t, y], rank_sem.at[k]
            there = members.at[0, pl.ds(pl.multiple_of(t * GROUP + y * SLOTS, SLOTS), SLOTS)]
            there_sem = member_sem.at[k]
            target = place(ax, ay, az, core)

            def away():
                remote(out_rank.at[c], rank_there, rank_send_sem, rank_there_sem, target).start()
                remote(outgoing.at[c], there, send_sem, there_sem, target).start()

            if (dx, dz) == (0, 0):
                pl.when(ay != y)(away)

                @pl.when(ay == y)
                def _():
                    pltpu.make_async_copy(out_rank.at[c], rank_there, rank_there_sem).start()
                    pltpu.make_async_copy(outgoing.at[c], there, there_sem).start()
            else:
                away()

    @pl.when(jnp.logical_not(holds))
    def _():
        for side, (dx, dz) in enumerate(RELAYED):
            t = ORDER.index((dx, dz))
            k = step_of(t)
            target = place((x + 4 - dx) % 4, y, z, core)
            arrived(passing_rank.at[side], pass_rank_sem.at[side])
            remote(
                passing_rank.at[side], member_rank.at[0, t], pass_rank_send_sem, rank_sem.at[k], target
            ).start()
            arrived(passing.at[side], pass_sem.at[side])
            for sy in range(4):
                remote(
                    passing.at[side, sy], members.at[0, pl.ds(t * GROUP + sy * SLOTS, SLOTS)], pass_send_sem,
                    member_sem.at[k], target,
                ).start()

    @pl.when(holds)
    def _():
        best[...] = jnp.full(best.shape, -1.0, jnp.float32)
        sibling = place(x, y, z, 1 - core)

        def scores(side, j0, j1, i0, i1):
            if j0 == j1 or i0 == i1:
                return
            js, iss = pl.ds(j0 * GROUP, (j1 - j0) * GROUP), pl.ds(i0 * GROUP, (i1 - i0) * GROUP)
            found = lax.dot_general(
                members[side, js], members[0, iss], contract_last, preferred_element_type=jnp.float32
            )
            column = jnp.concatenate([rank_column[side, js]] * (i1 - i0), axis=1)
            found = jnp.where(column < rank_row[:, iss], found, -1.0)
            found = jnp.max(found.reshape((j1 - j0) * GROUP // 8, 8, (i1 - i0) * GROUP), axis=0)
            best[:, iss] = jnp.maximum(best[:, iss], found)

        def ranks(side, t0, t1):
            for t in range(t0, t1):
                row = jnp.sum(member_rank[side, t].reshape(4, GROUP), axis=0, keepdims=True)
                if side == 0:
                    rank_row[:, pl.ds(t * GROUP, GROUP)] = row
                rank_column[side, pl.ds(t * GROUP, GROUP)] = jnp.broadcast_to(row, (GROUP, GROUP)).T

        def part(ref, k, side):
            if ref is member_rank:
                return ref.at[side, pl.ds(STARTS[k], STEPS[k])]
            return ref.at[side, pl.ds(STARTS[k] * GROUP, STEPS[k] * GROUP)]

        last = len(STEPS)
        for k in range(last + 1):
            if k < last:
                arrived(part(member_rank, k, 0), rank_sem.at[k])
                remote(
                    part(member_rank, k, 0), part(member_rank, k, 1), pair_rank_send_sem, pair_rank_sem.at[k],
                    sibling,
                ).start()
                arrived(part(members, k, 0), member_sem.at[k])
                remote(
                    part(members, k, 0), part(members, k, 1), pair_send_sem, pair_sem.at[k], sibling
                ).start()
                s, e = STARTS[k], STARTS[k + 1]
                ranks(0, s, e)
                scores(0, s, e, 0, s)
                scores(0, 0, e, s, e)
            else:
                s, e = GROUPS, GROUPS
            if k > 0:
                p, q = STARTS[k - 1], STARTS[k]
                scores(1, 0, p, s, e)
                arrived(part(member_rank, k - 1, 1), pair_rank_sem.at[k - 1])
                arrived(part(members, k - 1, 1), pair_sem.at[k - 1])
                ranks(1, p, q)
                scores(1, p, q, 0, e)

        for t, (dx, dz) in enumerate(ORDER):
            mine_here = best.at[:, pl.ds(t * GROUP, GROUP)]
            for sy in range(4):
                target = place((x + dx) % 4, sy, (z + dz) % 4, core)

                def away():
                    remote(mine_here, back.at[own], back_send_sem, back_sem, target).start()

                if (dx, dz) == (0, 0):
                    pl.when(sy != y)(away)

                    @pl.when(sy == y)
                    def _():
                        pltpu.make_async_copy(mine_here, back.at[own], back_sem).start()
                else:
                    away()

    arrived(back, back_sem)
    table = jnp.max(back[...], axis=1)
    found = lax.dot_general(
        table, onehot, (((0,), (0,)), ((), ())),
        precision=lax.Precision.HIGHEST, preferred_element_type=jnp.float32,
    )
    out_ref[...] = jnp.sum(jnp.where(lane_hit, found, 0.0), axis=0, keepdims=True)

    @pl.when(holds)
    def _():
        arrived(outgoing.at[pl.ds(0, CLUSTERS - 1)], send_sem)
        arrived(out_rank.at[pl.ds(0, CLUSTERS - 1)], rank_send_sem)
        arrived(members.at[0], pair_send_sem)
        arrived(member_rank.at[0], pair_rank_send_sem)
        arrived(back, back_send_sem)
        arrived(back.at[pl.ds(0, CLUSTERS - 1)], back_send_sem)

    @pl.when(jnp.logical_not(holds))
    def _():
        arrived(outgoing, send_sem)
        arrived(out_rank, rank_send_sem)
        arrived(passing, pass_send_sem)
        arrived(passing_rank, pass_rank_send_sem)


def body(embedding, cluster, rank):
    rows, width = embedding.shape
    vmem = pl.BlockSpec(memory_space=pltpu.VMEM)
    dma = pltpu.SemaphoreType.DMA
    steps = len(STEPS)
    found = pl.pallas_call(
        kernel,
        out_shape=jax.ShapeDtypeStruct((1, rows), jnp.float32),
        in_specs=[vmem] * 3,
        out_specs=vmem,
        scratch_shapes=[
            pltpu.VMEM((CLUSTERS, SLOTS, width), jnp.bfloat16),
            pltpu.VMEM((CLUSTERS, 1, GROUP), jnp.float32),
            pltpu.VMEM((2, 4, SLOTS, width), jnp.bfloat16),
            pltpu.VMEM((2, 4, 1, GROUP), jnp.float32),
            pltpu.VMEM((2, GROUPS * GROUP, width), jnp.bfloat16),
            pltpu.VMEM((2, GROUPS, 4, 1, GROUP), jnp.float32),
            pltpu.VMEM((2, GROUPS * GROUP, GROUP), jnp.float32),
            pltpu.VMEM((1, GROUPS * GROUP), jnp.float32),
            pltpu.VMEM((8, GROUPS * GROUP), jnp.float32),
            pltpu.VMEM((CLUSTERS, 8, GROUP), jnp.float32),
            dma, dma, dma((2,)), dma((2,)), dma, dma, dma((steps,)), dma((steps,)),
            dma, dma, dma((steps,)), dma((steps,)), dma, dma,
        ],
        compiler_params=pltpu.CompilerParams(
            collective_id=0, has_side_effects=True, vmem_limit_bytes=56 << 20
        ),
    )(embedding, cluster.reshape(1, rows), rank.reshape(1, rows))
    return found.reshape(rows)


def solution(mesh):
    return jax.shard_map(
        body,
        mesh=mesh,
        in_specs=(P(("shard", "split"), None), P(("shard", "split")), P(("shard", "split"))),
        out_specs=P(("shard", "split")),
        check_vma=False,
    )
```

```python
import jax
import jax.numpy as jnp
from jax import lax
from jax.experimental import pallas as pl
from jax.experimental.pallas import tpu as pltpu
from jax.sharding import PartitionSpec as P

MESH = pl.DeviceIdType.MESH
CLUSTERS = 32
SLOTS = 32
GROUP = 4 * SLOTS
GROUPS = 16
PARITY = 0
NO_RANK = float(1 << 30)
ORDER = [
    (0, 0), (1, 0), (3, 0), (2, 0), (0, 1), (1, 1), (3, 1), (2, 1),
    (0, 3), (3, 3), (0, 2), (1, 2), (3, 2), (1, 3), (2, 2), (2, 3),
]
RELAYED = {(1, 3): 1, (2, 2): 3, (2, 3): 1}
SENDS = list(RELAYED) + [d for d in ORDER[::-1] if d not in RELAYED]
STEPS = [4, 4, 4, 2, 2]
STARTS = [sum(STEPS[:k]) for k in range(len(STEPS) + 1)]


def place(x, y, z, core):
    return (2 * x + core, 4 * z + y)


def turned(dz, odd):
    return dz if dz % 2 == 0 else (dz + 2 * odd) % 4


def step_of(t):
    return max(k for k in range(len(STEPS)) if STARTS[k] <= t)


def arrived(ref, sem):
    pltpu.make_async_copy(ref, ref, sem).wait()


def remote(src, dst, send_sem, recv_sem, target):
    return pltpu.make_async_remote_copy(
        src, dst, send_sem, recv_sem, device_id=target, device_id_type=MESH
    )


def kernel(
    embedding_any, cluster_any, rank_any, out_ref,
    embedding_ref, cluster_ref, rank_ref, outgoing, out_rank, passing, members, member_rank, rank_column, rank_row, best, reply, back,
    load_sem, send_sem, rank_send_sem, pass_sem, pass_send_sem, member_sem, rank_sem,
    pair_send_sem, pair_rank_send_sem, pair_sem, pair_rank_sem, back_send_sem, back_sem,
):
    shard, split = lax.axis_index("shard"), lax.axis_index("split")
    x, core, z, y = shard // 2, shard % 2, split // 4, split % 4
    holds = (x + y + z) % 2 == PARITY
    own = x + 4 * y + 16 * (z // 2)
    rows = embedding_ref.shape[0]
    loads = [
        pltpu.make_async_copy(src, dst, load_sem.at[n])
        for n, (src, dst) in enumerate(
            [(embedding_any, embedding_ref), (cluster_any, cluster_ref), (rank_any, rank_ref)]
        )
    ]
    for load in loads:
        load.start()

    barrier = pltpu.get_barrier_semaphore()

    def greet(gx, gy, gz, gcore):
        pl.semaphore_signal(barrier, inc=1, device_id=place(gx, gy, gz, gcore), device_id_type=MESH)

    @pl.when(holds)
    def _():
        def each(s, carry):
            greet(s % 4, (s // 4) % 4, s // 16, core)
            return carry

        lax.fori_loop(0, 64, each, 0)
        greet(x, y, z, 1 - core)

    @pl.when(jnp.logical_not(holds))
    def _():
        for (dx, dz), aside in RELAYED.items():
            for sy in range(4):
                greet((x + 4 - aside + dx) % 4, sy, (z + turned(dz, z % 2)) % 4, core)

    for load in loads:
        load.wait()
    values = embedding_ref[...].astype(jnp.float32)
    unit = (
        values * lax.rsqrt(jnp.sum(values * values, axis=1, keepdims=True) + 1e-06)
    ).astype(jnp.bfloat16)
    cluster = cluster_ref[...]
    rank = rank_ref[...]
    cluster_hit = lax.broadcasted_iota(jnp.int32, (CLUSTERS, rows), 0) == cluster
    onehot = cluster_hit.astype(jnp.float32)
    earlier = (
        lax.broadcasted_iota(jnp.int32, (rows, rows), 0) < lax.broadcasted_iota(jnp.int32, (rows, rows), 1)
    ).astype(jnp.float32).astype(jnp.bfloat16)
    before = jnp.dot(onehot.astype(jnp.bfloat16), earlier, preferred_element_type=jnp.float32)
    position = jnp.sum(before * onehot, axis=0, keepdims=True).astype(jnp.int32)
    slot = cluster * SLOTS + position

    def fill(part, carry):
        pick = (
            lax.broadcasted_iota(jnp.int32, (256, rows), 0) + part * 256 == slot
        ).astype(jnp.float32).astype(jnp.bfloat16)
        packed = jnp.dot(pick, unit, preferred_element_type=jnp.float32).astype(jnp.bfloat16)
        outgoing[pl.ds(part * 8, 8)] = packed.reshape(8, SLOTS, packed.shape[1])
        return carry

    lax.fori_loop(0, CLUSTERS * SLOTS // 256, fill, 0)

    lane_hit = lax.broadcasted_iota(jnp.int32, (GROUP, rows), 0) == position + SLOTS * y
    lane_onehot = lane_hit.astype(jnp.float32).astype(jnp.bfloat16)
    contract_last = (((1,), (1,)), ((), ()))

    def spread(part):
        return lax.dot_general(
            (onehot * part.astype(jnp.float32)).astype(jnp.bfloat16), lane_onehot, contract_last,
            preferred_element_type=jnp.float32,
        )

    taken = spread(jnp.ones_like(rank))
    slot_rank = (
        spread(rank % 128) + 128.0 * spread(rank // 128 % 128) + 16384.0 * spread(rank // 16384)
    )
    mine = lax.broadcasted_iota(jnp.int32, (CLUSTERS, GROUP), 1) // SLOTS == y
    out_rank[...] = jnp.where(mine, jnp.where(taken > 0.5, slot_rank, NO_RANK), 0.0).reshape(CLUSTERS, 1, GROUP)

    pl.semaphore_wait(barrier, CLUSTERS + 2 * len(RELAYED) + jnp.where(holds, 1, 0))

    for dx, dz in SENDS:
        ax, az = (x + 4 - dx) % 4, (z + 4 - turned(dz, (z + dz) % 2)) % 4
        for half in range(2):
            ay = (y + (ax + y + az + PARITY) % 2 + 2 * half) % 4
            c = ax + 4 * ay + 16 * (az // 2)
            there = member_rank.at[0, ORDER.index((dx, dz)), y]

            def away():
                remote(out_rank.at[c], there, rank_send_sem, rank_sem, place(ax, ay, az, core)).start()

            if (dx, dz) == (0, 0):
                pl.when(ay != y)(away)

                @pl.when(ay == y)
                def _():
                    pltpu.make_async_copy(out_rank.at[c], there, rank_sem).start()
            else:
                away()

    for dx, dz in SENDS:
        t = ORDER.index((dx, dz))
        ax, az = (x + 4 - dx) % 4, (z + 4 - turned(dz, (z + dz) % 2)) % 4
        for half in range(2):
            ay = (y + (ax + y + az + PARITY) % 2 + 2 * half) % 4
            c = ax + 4 * ay + 16 * (az // 2)
            if (dx, dz) in RELAYED:
                side = list(RELAYED).index((dx, dz))
                target = place((ax + RELAYED[dx, dz]) % 4, ay, az, core)
                remote(outgoing.at[c], passing.at[side, y], send_sem, pass_sem.at[side, y], target).start()
                continue
            k = step_of(t)
            there = members.at[0, pl.ds(pl.multiple_of(t * GROUP + y * SLOTS, SLOTS), SLOTS)]
            there_sem = member_sem.at[k]
            target = place(ax, ay, az, core)

            def away():
                remote(outgoing.at[c], there, send_sem, there_sem, target).start()

            if (dx, dz) == (0, 0):
                pl.when(ay != y)(away)

                @pl.when(ay == y)
                def _():
                    pltpu.make_async_copy(outgoing.at[c], there, there_sem).start()
            else:
                away()

    @pl.when(jnp.logical_not(holds))
    def _():
        for side, ((dx, dz), aside) in enumerate(RELAYED.items()):
            t = ORDER.index((dx, dz))
            target = place((x + 4 - aside) % 4, y, z, core)
            for sy in range(4):
                arrived(passing.at[side, sy], pass_sem.at[side, sy])
                remote(
                    passing.at[side, sy], members.at[0, pl.ds(t * GROUP + sy * SLOTS, SLOTS)], pass_send_sem,
                    member_sem.at[step_of(t)], target,
                ).start()

    @pl.when(holds)
    def _():
        best[...] = jnp.full(best.shape, -1.0, jnp.float32)
        sibling = place(x, y, z, 1 - core)

        def scores(side, j0, j1, i0, i1):
            if j0 == j1 or i0 == i1:
                return
            js, iss = pl.ds(j0 * GROUP, (j1 - j0) * GROUP), pl.ds(i0 * GROUP, (i1 - i0) * GROUP)
            found = lax.dot_general(
                members[side, js], members[0, iss], contract_last, preferred_element_type=jnp.float32
            )
            column = jnp.concatenate([rank_column[side, js]] * (i1 - i0), axis=1)
            found = jnp.where(column < rank_row[:, iss], found, -1.0)
            found = jnp.max(found.reshape((j1 - j0) * GROUP // 8, 8, (i1 - i0) * GROUP), axis=0)
            best[:, iss] = jnp.maximum(best[:, iss], found)

        def ranks(side):
            for t in range(GROUPS):
                row = jnp.sum(member_rank[side, t].reshape(4, GROUP), axis=0, keepdims=True)
                if side == 0:
                    rank_row[:, pl.ds(t * GROUP, GROUP)] = row
                rank_column[side, pl.ds(t * GROUP, GROUP)] = jnp.broadcast_to(row, (GROUP, GROUP)).T

        def part(k, side):
            return members.at[side, pl.ds(STARTS[k] * GROUP, STEPS[k] * GROUP)]

        arrived(member_rank.at[0], rank_sem)
        remote(member_rank.at[0], member_rank.at[1], pair_rank_send_sem, pair_rank_sem, sibling).start()
        ranks(0)
        arrived(member_rank.at[1], pair_rank_sem)
        ranks(1)

        last = len(STEPS)
        for k in range(last + 1):
            if k < last:
                arrived(part(k, 0), member_sem.at[k])
                remote(part(k, 0), part(k, 1), pair_send_sem, pair_sem.at[k], sibling).start()
                s, e = STARTS[k], STARTS[k + 1]
                scores(0, s, e, 0, s)
                scores(0, 0, e, s, e)
            else:
                s, e = GROUPS, GROUPS
            if k > 0:
                p, q = STARTS[k - 1], STARTS[k]
                scores(1, 0, p, s, e)
                arrived(part(k - 1, 1), pair_sem.at[k - 1])
                scores(1, p, q, 0, e)

        for t, (dx, dz) in enumerate(ORDER):
            reply[t] = jnp.max(best[:, pl.ds(t * GROUP, GROUP)], axis=0, keepdims=True)
            for sy in range(4):
                target = place((x + dx) % 4, sy, (z + turned(dz, z % 2)) % 4, core)

                def away():
                    remote(reply.at[t], back.at[own], back_send_sem, back_sem, target).start()

                if (dx, dz) == (0, 0):
                    pl.when(sy != y)(away)

                    @pl.when(sy == y)
                    def _():
                        pltpu.make_async_copy(reply.at[t], back.at[own], back_sem).start()
                else:
                    away()

    arrived(back, back_sem)
    table = back[...].reshape(CLUSTERS, GROUP)
    found = lax.dot_general(
        table, onehot, (((0,), (0,)), ((), ())),
        precision=lax.Precision.HIGHEST, preferred_element_type=jnp.float32,
    )
    out_ref[...] = jnp.sum(jnp.where(lane_hit, found, 0.0), axis=0, keepdims=True)

    @pl.when(holds)
    def _():
        arrived(outgoing.at[pl.ds(0, CLUSTERS - 1)], send_sem)
        arrived(out_rank.at[pl.ds(0, CLUSTERS - 1)], rank_send_sem)
        arrived(members.at[0], pair_send_sem)
        arrived(member_rank.at[0], pair_rank_send_sem)
        arrived(back, back_send_sem)
        arrived(back.at[pl.ds(0, CLUSTERS - 1)], back_send_sem)

    @pl.when(jnp.logical_not(holds))
    def _():
        arrived(outgoing, send_sem)
        arrived(out_rank, rank_send_sem)
        arrived(passing, pass_send_sem)


def body(embedding, cluster, rank):
    rows, width = embedding.shape
    vmem = pl.BlockSpec(memory_space=pltpu.VMEM)
    dma = pltpu.SemaphoreType.DMA
    steps = len(STEPS)
    found = pl.pallas_call(
        kernel,
        out_shape=jax.ShapeDtypeStruct((1, rows), jnp.float32),
        in_specs=[pl.BlockSpec(memory_space=pl.ANY)] * 3,
        out_specs=vmem,
        scratch_shapes=[
            pltpu.VMEM((rows, width), jnp.bfloat16),
            pltpu.VMEM((1, rows), jnp.int32),
            pltpu.VMEM((1, rows), jnp.int32),
            pltpu.VMEM((CLUSTERS, SLOTS, width), jnp.bfloat16),
            pltpu.VMEM((CLUSTERS, 1, GROUP), jnp.float32),
            pltpu.VMEM((len(RELAYED), 4, SLOTS, width), jnp.bfloat16),
            pltpu.VMEM((2, GROUPS * GROUP, width), jnp.bfloat16),
            pltpu.VMEM((2, GROUPS, 4, 1, GROUP), jnp.float32),
            pltpu.VMEM((2, GROUPS * GROUP, GROUP), jnp.float32),
            pltpu.VMEM((1, GROUPS * GROUP), jnp.float32),
            pltpu.VMEM((8, GROUPS * GROUP), jnp.float32),
            pltpu.VMEM((GROUPS, 1, GROUP), jnp.float32),
            pltpu.VMEM((CLUSTERS, 1, GROUP), jnp.float32),
            dma((3,)), dma, dma, dma((len(RELAYED), 4)), dma, dma((steps,)), dma,
            dma, dma, dma((steps,)), dma, dma, dma,
        ],
        compiler_params=pltpu.CompilerParams(
            collective_id=0, has_side_effects=True, vmem_limit_bytes=56 << 20
        ),
    )(embedding, cluster.reshape(1, rows), rank.reshape(1, rows))
    return found.reshape(rows)


def solution(mesh):
    return jax.shard_map(
        body,
        mesh=mesh,
        in_specs=(P(("shard", "split"), None), P(("shard", "split")), P(("shard", "split"))),
        out_specs=P(("shard", "split")),
        check_vma=False,
    )
```

```python
import jax
import jax.numpy as jnp
from jax import lax
from jax.experimental import pallas as pl
from jax.experimental.pallas import tpu as pltpu
from jax.sharding import PartitionSpec as P

MESH = pl.DeviceIdType.MESH
CLUSTERS = 32
SLOTS = 32
GROUP = 4 * SLOTS
GROUPS = 16
PARITY = 0
NO_RANK = float(1 << 30)
ORDER = [
    (0, 0), (1, 0), (3, 0), (2, 0), (0, 1), (1, 1), (3, 1), (2, 1),
    (1, 3), (3, 3), (0, 2), (1, 2), (3, 2), (2, 3), (2, 2), (0, 3),
]
RELAYED = {(2, 3): 3, (2, 2): 1, (0, 3): 3}
SENDS = list(RELAYED) + [d for d in ORDER[::-1] if d not in RELAYED]
STEPS = [8, 4, 4]
STARTS = [sum(STEPS[:k]) for k in range(len(STEPS) + 1)]


def place(x, y, z, core):
    return (2 * x + core, 4 * z + y)


def turned(dz, odd):
    return dz if dz % 2 == 0 else (dz + 2 * odd) % 4


def step_of(t):
    return max(k for k in range(len(STEPS)) if STARTS[k] <= t)


def arrived(ref, sem):
    pltpu.make_async_copy(ref, ref, sem).wait()


def remote(src, dst, send_sem, recv_sem, target):
    return pltpu.make_async_remote_copy(
        src, dst, send_sem, recv_sem, device_id=target, device_id_type=MESH
    )


def kernel(
    embedding_any, cluster_any, rank_any, out_ref,
    embedding_ref, cluster_ref, rank_ref, outgoing, out_rank, passing, members, member_rank, rank_column, rank_row, best, turned_best, reply, back,
    load_sem, send_sem, rank_send_sem, pass_sem, pass_send_sem, member_sem, rank_sem,
    pair_send_sem, pair_rank_send_sem, pair_sem, pair_rank_sem, back_send_sem, back_sem,
):
    shard, split = lax.axis_index("shard"), lax.axis_index("split")
    x, core, z, y = shard // 2, shard % 2, split // 4, split % 4
    holds = (x + y + z) % 2 == PARITY
    own = x + 4 * y + 16 * (z // 2)
    rows = embedding_ref.shape[0]
    loads = [
        pltpu.make_async_copy(src, dst, load_sem.at[n])
        for n, (src, dst) in enumerate(
            [(embedding_any, embedding_ref), (cluster_any, cluster_ref), (rank_any, rank_ref)]
        )
    ]
    for load in loads:
        load.start()

    barrier = pltpu.get_barrier_semaphore()

    def greet(gx, gy, gz, gcore):
        pl.semaphore_signal(barrier, inc=1, device_id=place(gx, gy, gz, gcore), device_id_type=MESH)

    @pl.when(holds)
    def _():
        def each(s, carry):
            greet(s % 4, (s // 4) % 4, s // 16, core)
            return carry

        lax.fori_loop(0, 64, each, 0)
        greet(x, y, z, 1 - core)

    @pl.when(jnp.logical_not(holds))
    def _():
        for (dx, dz), aside in RELAYED.items():
            for sy in range(4):
                greet((x + 4 - aside + dx) % 4, sy, (z + turned(dz, z % 2)) % 4, core)

    for load in loads:
        load.wait()
    values = embedding_ref[...].astype(jnp.float32)
    unit = (
        values * lax.rsqrt(jnp.sum(values * values, axis=1, keepdims=True) + 1e-06)
    ).astype(jnp.bfloat16)
    cluster = cluster_ref[...]
    rank = rank_ref[...]
    cluster_hit = lax.broadcasted_iota(jnp.int32, (CLUSTERS, rows), 0) == cluster
    onehot = cluster_hit.astype(jnp.float32)
    earlier = (
        lax.broadcasted_iota(jnp.int32, (rows, rows), 0) < lax.broadcasted_iota(jnp.int32, (rows, rows), 1)
    ).astype(jnp.float32).astype(jnp.bfloat16)
    before = jnp.dot(onehot.astype(jnp.bfloat16), earlier, preferred_element_type=jnp.float32)
    position = jnp.sum(before * onehot, axis=0, keepdims=True).astype(jnp.int32)
    slot = cluster * SLOTS + position

    def fill(part, carry):
        pick = (
            lax.broadcasted_iota(jnp.int32, (256, rows), 0) + part * 256 == slot
        ).astype(jnp.float32).astype(jnp.bfloat16)
        packed = jnp.dot(pick, unit, preferred_element_type=jnp.float32).astype(jnp.bfloat16)
        outgoing[pl.ds(part * 8, 8)] = packed.reshape(8, SLOTS, packed.shape[1])
        return carry

    lax.fori_loop(0, CLUSTERS * SLOTS // 256, fill, 0)

    lane_hit = lax.broadcasted_iota(jnp.int32, (GROUP, rows), 0) == position + SLOTS * y
    lane_onehot = lane_hit.astype(jnp.float32).astype(jnp.bfloat16)
    contract_last = (((1,), (1,)), ((), ()))

    def spread(part):
        return lax.dot_general(
            (onehot * part.astype(jnp.float32)).astype(jnp.bfloat16), lane_onehot, contract_last,
            preferred_element_type=jnp.float32,
        )

    taken = spread(jnp.ones_like(rank))
    slot_rank = (
        spread(rank % 128) + 128.0 * spread(rank // 128 % 128) + 16384.0 * spread(rank // 16384)
    )
    mine = lax.broadcasted_iota(jnp.int32, (CLUSTERS, GROUP), 1) // SLOTS == y
    out_rank[...] = jnp.where(mine, jnp.where(taken > 0.5, slot_rank, NO_RANK), 0.0).reshape(CLUSTERS, 1, GROUP)

    pl.semaphore_wait(barrier, CLUSTERS + 2 * len(RELAYED) + jnp.where(holds, 1, 0))

    for dx, dz in SENDS:
        ax, az = (x + 4 - dx) % 4, (z + 4 - turned(dz, (z + dz) % 2)) % 4
        for half in range(2):
            ay = (y + (ax + y + az + PARITY) % 2 + 2 * half) % 4
            c = ax + 4 * ay + 16 * (az // 2)
            there = member_rank.at[0, ORDER.index((dx, dz)), y]

            def away():
                remote(out_rank.at[c], there, rank_send_sem, rank_sem, place(ax, ay, az, core)).start()

            if (dx, dz) == (0, 0):
                pl.when(ay != y)(away)

                @pl.when(ay == y)
                def _():
                    pltpu.make_async_copy(out_rank.at[c], there, rank_sem).start()
            else:
                away()

    for dx, dz in SENDS:
        t = ORDER.index((dx, dz))
        ax, az = (x + 4 - dx) % 4, (z + 4 - turned(dz, (z + dz) % 2)) % 4
        for half in range(2):
            ay = (y + (ax + y + az + PARITY) % 2 + 2 * half) % 4
            c = ax + 4 * ay + 16 * (az // 2)
            if (dx, dz) in RELAYED:
                side = list(RELAYED).index((dx, dz))
                target = place((ax + RELAYED[dx, dz]) % 4, ay, az, core)
                remote(outgoing.at[c], passing.at[side, y], send_sem, pass_sem.at[side, y], target).start()
                continue
            k = step_of(t)
            there = members.at[0, pl.ds(pl.multiple_of(t * GROUP + y * SLOTS, SLOTS), SLOTS)]
            there_sem = member_sem.at[k]
            target = place(ax, ay, az, core)

            def away():
                remote(outgoing.at[c], there, send_sem, there_sem, target).start()

            if (dx, dz) == (0, 0):
                pl.when(ay != y)(away)

                @pl.when(ay == y)
                def _():
                    pltpu.make_async_copy(outgoing.at[c], there, there_sem).start()
            else:
                away()

    @pl.when(jnp.logical_not(holds))
    def _():
        for side, ((dx, dz), aside) in enumerate(RELAYED.items()):
            t = ORDER.index((dx, dz))
            target = place((x + 4 - aside) % 4, y, z, core)
            for sy in range(4):
                arrived(passing.at[side, sy], pass_sem.at[side, sy])
                remote(
                    passing.at[side, sy], members.at[0, pl.ds(t * GROUP + sy * SLOTS, SLOTS)], pass_send_sem,
                    member_sem.at[step_of(t)], target,
                ).start()

    @pl.when(holds)
    def _():
        best[...] = jnp.full(best.shape, -1.0, jnp.float32)
        turned_best[...] = jnp.full(turned_best.shape, -1.0, jnp.float32)
        sibling = place(x, y, z, 1 - core)

        def scores(side, j0, j1, i0, i1):
            if j0 == j1 or i0 == i1:
                return
            js, iss = pl.ds(j0 * GROUP, (j1 - j0) * GROUP), pl.ds(i0 * GROUP, (i1 - i0) * GROUP)
            found = lax.dot_general(
                members[side, js], members[0, iss], contract_last, preferred_element_type=jnp.float32
            )
            column = jnp.concatenate([rank_column[side, js]] * (i1 - i0), axis=1)
            found = jnp.where(column < rank_row[:, iss], found, -1.0)
            found = jnp.max(found.reshape((j1 - j0) * GROUP // 8, 8, (i1 - i0) * GROUP), axis=0)
            best[:, iss] = jnp.maximum(best[:, iss], found)

        def both(j0, j1, i0, i1):
            if j0 == j1 or i0 == i1:
                return
            js, iss = pl.ds(j0 * GROUP, (j1 - j0) * GROUP), pl.ds(i0 * GROUP, (i1 - i0) * GROUP)
            found = lax.dot_general(
                members[0, js], members[0, iss], contract_last, preferred_element_type=jnp.float32
            )
            column = jnp.concatenate([rank_column[0, js]] * (i1 - i0), axis=1)
            row = rank_row[:, iss]
            down = jnp.max(
                jnp.where(column < row, found, -1.0).reshape((j1 - j0) * GROUP // 8, 8, (i1 - i0) * GROUP), axis=0
            )
            best[:, iss] = jnp.maximum(best[:, iss], down)
            across = jnp.where(row < column, found, -1.0)
            parts = [across[:, GROUP * n : GROUP * (n + 1)] for n in range(i1 - i0)]
            while len(parts) > 1:
                parts = [jnp.maximum(a, b) for a, b in zip(parts[::2], parts[1::2])] + parts[len(parts) // 2 * 2 :]
            turned_best[js] = jnp.maximum(turned_best[js], parts[0])

        def ranks(side):
            for t in range(GROUPS):
                row = jnp.sum(member_rank[side, t].reshape(4, GROUP), axis=0, keepdims=True)
                if side == 0:
                    rank_row[:, pl.ds(t * GROUP, GROUP)] = row
                rank_column[side, pl.ds(t * GROUP, GROUP)] = jnp.broadcast_to(row, (GROUP, GROUP)).T

        def part(k, side):
            return members.at[side, pl.ds(STARTS[k] * GROUP, STEPS[k] * GROUP)]

        arrived(member_rank.at[0], rank_sem)
        remote(member_rank.at[0], member_rank.at[1], pair_rank_send_sem, pair_rank_sem, sibling).start()
        ranks(0)
        arrived(member_rank.at[1], pair_rank_sem)
        ranks(1)

        last = len(STEPS)
        for k in range(last + 1):
            s, e = (STARTS[k], STARTS[k + 1]) if k < last else (GROUPS, GROUPS)
            if k < last:
                arrived(part(k, 0), member_sem.at[k])
                remote(part(k, 0), part(k, 1), pair_send_sem, pair_sem.at[k], sibling).start()
            if k > 0:
                p, q = STARTS[k - 1], STARTS[k]
                arrived(part(k - 1, 1), pair_sem.at[k - 1])
                scores(1, p, q, 0, e)
                scores(1, 0, p, s, e)
                if k == last:
                    for t in range(p):
                        lanes = pl.ds(t * GROUP, GROUP)
                        other = jnp.max(turned_best[lanes].T.reshape(GROUP // 8, 8, GROUP), axis=0)
                        best[:, lanes] = jnp.maximum(best[:, lanes], other)
            if k < last:
                both(0, s, s, e)
                scores(0, s, e, s, e)

        for t, (dx, dz) in enumerate(ORDER):
            reply[t] = jnp.max(best[:, pl.ds(t * GROUP, GROUP)], axis=0, keepdims=True)
            for sy in range(4):
                target = place((x + dx) % 4, sy, (z + turned(dz, z % 2)) % 4, core)

                def away():
                    remote(reply.at[t], back.at[own], back_send_sem, back_sem, target).start()

                if (dx, dz) == (0, 0):
                    pl.when(sy != y)(away)

                    @pl.when(sy == y)
                    def _():
                        pltpu.make_async_copy(reply.at[t], back.at[own], back_sem).start()
                else:
                    away()

    arrived(back, back_sem)
    table = back[...].reshape(CLUSTERS, GROUP)
    found = lax.dot_general(
        table, onehot, (((0,), (0,)), ((), ())),
        precision=lax.Precision.HIGHEST, preferred_element_type=jnp.float32,
    )
    out_ref[...] = jnp.sum(jnp.where(lane_hit, found, 0.0), axis=0, keepdims=True)

    @pl.when(holds)
    def _():
        arrived(outgoing.at[pl.ds(0, CLUSTERS - 1)], send_sem)
        arrived(out_rank.at[pl.ds(0, CLUSTERS - 1)], rank_send_sem)
        arrived(members.at[0], pair_send_sem)
        arrived(member_rank.at[0], pair_rank_send_sem)
        arrived(back, back_send_sem)
        arrived(back.at[pl.ds(0, CLUSTERS - 1)], back_send_sem)

    @pl.when(jnp.logical_not(holds))
    def _():
        arrived(outgoing, send_sem)
        arrived(out_rank, rank_send_sem)
        arrived(passing, pass_send_sem)


def body(embedding, cluster, rank):
    rows, width = embedding.shape
    vmem = pl.BlockSpec(memory_space=pltpu.VMEM)
    dma = pltpu.SemaphoreType.DMA
    steps = len(STEPS)
    found = pl.pallas_call(
        kernel,
        out_shape=jax.ShapeDtypeStruct((1, rows), jnp.float32),
        in_specs=[pl.BlockSpec(memory_space=pl.ANY)] * 3,
        out_specs=vmem,
        scratch_shapes=[
            pltpu.VMEM((rows, width), jnp.bfloat16),
            pltpu.VMEM((1, rows), jnp.int32),
            pltpu.VMEM((1, rows), jnp.int32),
            pltpu.VMEM((CLUSTERS, SLOTS, width), jnp.bfloat16),
            pltpu.VMEM((CLUSTERS, 1, GROUP), jnp.float32),
            pltpu.VMEM((len(RELAYED), 4, SLOTS, width), jnp.bfloat16),
            pltpu.VMEM((2, GROUPS * GROUP, width), jnp.bfloat16),
            pltpu.VMEM((2, GROUPS, 4, 1, GROUP), jnp.float32),
            pltpu.VMEM((2, GROUPS * GROUP, GROUP), jnp.float32),
            pltpu.VMEM((1, GROUPS * GROUP), jnp.float32),
            pltpu.VMEM((8, GROUPS * GROUP), jnp.float32),
            pltpu.VMEM((STARTS[-2] * GROUP, GROUP), jnp.float32),
            pltpu.VMEM((GROUPS, 1, GROUP), jnp.float32),
            pltpu.VMEM((CLUSTERS, 1, GROUP), jnp.float32),
            dma((3,)), dma, dma, dma((len(RELAYED), 4)), dma, dma((steps,)), dma,
            dma, dma, dma((steps,)), dma, dma, dma,
        ],
        compiler_params=pltpu.CompilerParams(
            collective_id=0, has_side_effects=True, vmem_limit_bytes=56 << 20
        ),
    )(embedding, cluster.reshape(1, rows), rank.reshape(1, rows))
    return found.reshape(rows)


def solution(mesh):
    return jax.shard_map(
        body,
        mesh=mesh,
        in_specs=(P(("shard", "split"), None), P(("shard", "split")), P(("shard", "split"))),
        out_specs=P(("shard", "split")),
        check_vma=False,
    )
```

```python
import jax
import jax.numpy as jnp
from jax import lax
from jax.experimental import pallas as pl
from jax.experimental.pallas import tpu as pltpu
from jax.sharding import PartitionSpec as P

MESH = pl.DeviceIdType.MESH
CLUSTERS = 32
SLOTS = 32
GROUP = 4 * SLOTS
GROUPS = 16
PARITY = 0
NO_RANK = float(1 << 30)
ORDER = [
    (0, 0), (1, 0), (3, 0), (2, 0), (0, 1), (1, 1), (3, 1), (2, 1),
    (1, 3), (3, 3), (0, 2), (1, 2), (3, 2), (2, 3), (2, 2), (0, 3),
]
RELAYED = {(2, 3): 3, (2, 2): 1, (0, 3): 3}
SENDS = list(RELAYED) + [d for d in ORDER[::-1] if d not in RELAYED]
STEPS = [8, 4, 4]
STARTS = [sum(STEPS[:k]) for k in range(len(STEPS) + 1)]


def place(x, y, z, core):
    return (2 * x + core, 4 * z + y)


def turned(dz, odd):
    return dz if dz % 2 == 0 else (dz + 2 * odd) % 4


def step_of(t):
    return max(k for k in range(len(STEPS)) if STARTS[k] <= t)


def arrived(ref, sem):
    pltpu.make_async_copy(ref, ref, sem).wait()


def remote(src, dst, send_sem, recv_sem, target):
    return pltpu.make_async_remote_copy(
        src, dst, send_sem, recv_sem, device_id=target, device_id_type=MESH
    )


def kernel(
    embedding_any, cluster_any, rank_any, out_ref,
    embedding_ref, cluster_ref, rank_ref, outgoing, out_rank, passing, members, member_rank, rank_column, rank_row, best, turned_best, reply, back,
    load_sem, send_sem, rank_send_sem, pass_sem, pass_send_sem, member_sem, rank_sem,
    pair_send_sem, pair_rank_send_sem, pair_sem, pair_rank_sem, back_send_sem, back_sem,
):
    shard, split = lax.axis_index("shard"), lax.axis_index("split")
    x, core, z, y = shard // 2, shard % 2, split // 4, split % 4
    holds = (x + y + z) % 2 == PARITY
    own = x + 4 * y + 16 * (z // 2)
    rows = embedding_ref.shape[0]
    loads = [
        pltpu.make_async_copy(src, dst, load_sem.at[n])
        for n, (src, dst) in enumerate(
            [(embedding_any, embedding_ref), (cluster_any, cluster_ref), (rank_any, rank_ref)]
        )
    ]
    for load in loads:
        load.start()

    barrier = pltpu.get_barrier_semaphore()

    def greet(gx, gy, gz, gcore):
        pl.semaphore_signal(barrier, inc=1, device_id=place(gx, gy, gz, gcore), device_id_type=MESH)

    @pl.when(holds)
    def _():
        for s in range(64):
            greet(s % 4, s // 4 % 4, s // 16, core)
        greet(x, y, z, 1 - core)

    @pl.when(jnp.logical_not(holds))
    def _():
        for (dx, dz), aside in RELAYED.items():
            for sy in range(4):
                greet((x + 4 - aside + dx) % 4, sy, (z + turned(dz, z % 2)) % 4, core)

    for load in loads:
        load.wait()
    values = embedding_ref[...].astype(jnp.float32)
    unit = (
        values * lax.rsqrt(jnp.sum(values * values, axis=1, keepdims=True) + 1e-06)
    ).astype(jnp.bfloat16)
    cluster = cluster_ref[...]
    rank = rank_ref[...]
    cluster_hit = lax.broadcasted_iota(jnp.int32, (CLUSTERS, rows), 0) == cluster
    onehot = cluster_hit.astype(jnp.float32)
    earlier = (
        lax.broadcasted_iota(jnp.int32, (rows, rows), 0) < lax.broadcasted_iota(jnp.int32, (rows, rows), 1)
    ).astype(jnp.float32).astype(jnp.bfloat16)
    before = jnp.dot(onehot.astype(jnp.bfloat16), earlier, preferred_element_type=jnp.float32)
    position = jnp.sum(before * onehot, axis=0, keepdims=True).astype(jnp.int32)
    slot = cluster * SLOTS + position

    for part in range(CLUSTERS * SLOTS // 256):
        pick = (
            lax.broadcasted_iota(jnp.int32, (256, rows), 0) + part * 256 == slot
        ).astype(jnp.float32).astype(jnp.bfloat16)
        packed = jnp.dot(pick, unit, preferred_element_type=jnp.float32).astype(jnp.bfloat16)
        outgoing[pl.ds(part * 8, 8)] = packed.reshape(8, SLOTS, packed.shape[1])

    lane_hit = lax.broadcasted_iota(jnp.int32, (GROUP, rows), 0) == position + SLOTS * y
    lane_onehot = lane_hit.astype(jnp.float32).astype(jnp.bfloat16)
    contract_last = (((1,), (1,)), ((), ()))

    def spread(part):
        return lax.dot_general(
            (onehot * part.astype(jnp.float32)).astype(jnp.bfloat16), lane_onehot, contract_last,
            preferred_element_type=jnp.float32,
        )

    taken = spread(jnp.ones_like(rank))
    slot_rank = (
        spread(rank % 128) + 128.0 * spread(rank // 128 % 128) + 16384.0 * spread(rank // 16384)
    )
    mine = lax.broadcasted_iota(jnp.int32, (CLUSTERS, GROUP), 1) // SLOTS == y
    out_rank[...] = jnp.where(mine, jnp.where(taken > 0.5, slot_rank, NO_RANK), 0.0).reshape(CLUSTERS, 1, GROUP)

    pl.semaphore_wait(barrier, CLUSTERS + 2 * len(RELAYED) + jnp.where(holds, 1, 0))

    for dx, dz in SENDS:
        ax, az = (x + 4 - dx) % 4, (z + 4 - turned(dz, (z + dz) % 2)) % 4
        for half in range(2):
            ay = (y + (ax + y + az + PARITY) % 2 + 2 * half) % 4
            c = ax + 4 * ay + 16 * (az // 2)
            there = member_rank.at[0, ORDER.index((dx, dz)), y]

            def away():
                remote(out_rank.at[c], there, rank_send_sem, rank_sem, place(ax, ay, az, core)).start()

            if (dx, dz) == (0, 0):
                pl.when(ay != y)(away)

                @pl.when(ay == y)
                def _():
                    pltpu.make_async_copy(out_rank.at[c], there, rank_sem).start()
            else:
                away()

    for dx, dz in SENDS:
        t = ORDER.index((dx, dz))
        ax, az = (x + 4 - dx) % 4, (z + 4 - turned(dz, (z + dz) % 2)) % 4
        for half in range(2):
            ay = (y + (ax + y + az + PARITY) % 2 + 2 * half) % 4
            c = ax + 4 * ay + 16 * (az // 2)
            if (dx, dz) in RELAYED:
                side = list(RELAYED).index((dx, dz))
                target = place((ax + RELAYED[dx, dz]) % 4, ay, az, core)
                remote(outgoing.at[c], passing.at[side, y], send_sem, pass_sem.at[side, y], target).start()
                continue
            k = step_of(t)
            there = members.at[0, pl.ds(pl.multiple_of(t * GROUP + y * SLOTS, SLOTS), SLOTS)]
            there_sem = member_sem.at[k]
            target = place(ax, ay, az, core)

            def away():
                remote(outgoing.at[c], there, send_sem, there_sem, target).start()

            if (dx, dz) == (0, 0):
                pl.when(ay != y)(away)

                @pl.when(ay == y)
                def _():
                    pltpu.make_async_copy(outgoing.at[c], there, there_sem).start()
            else:
                away()

    @pl.when(jnp.logical_not(holds))
    def _():
        for side, ((dx, dz), aside) in enumerate(RELAYED.items()):
            t = ORDER.index((dx, dz))
            target = place((x + 4 - aside) % 4, y, z, core)
            for sy in range(4):
                arrived(passing.at[side, sy], pass_sem.at[side, sy])
                remote(
                    passing.at[side, sy], members.at[0, pl.ds(t * GROUP + sy * SLOTS, SLOTS)], pass_send_sem,
                    member_sem.at[step_of(t)], target,
                ).start()

    @pl.when(holds)
    def _():
        best[...] = jnp.full(best.shape, -1.0, jnp.float32)
        turned_best[...] = jnp.full(turned_best.shape, -1.0, jnp.float32)
        sibling = place(x, y, z, 1 - core)

        def scores(side, j0, j1, i0, i1):
            if j0 == j1 or i0 == i1:
                return
            js, iss = pl.ds(j0 * GROUP, (j1 - j0) * GROUP), pl.ds(i0 * GROUP, (i1 - i0) * GROUP)
            found = lax.dot_general(
                members[side, js], members[0, iss], contract_last, preferred_element_type=jnp.float32
            )
            column = jnp.concatenate([rank_column[side, js]] * (i1 - i0), axis=1)
            found = jnp.where(column < rank_row[:, iss], found, -1.0)
            found = jnp.max(found.reshape((j1 - j0) * GROUP // 8, 8, (i1 - i0) * GROUP), axis=0)
            best[:, iss] = jnp.maximum(best[:, iss], found)

        def both(j0, j1, i0, i1):
            if j0 == j1 or i0 == i1:
                return
            js, iss = pl.ds(j0 * GROUP, (j1 - j0) * GROUP), pl.ds(i0 * GROUP, (i1 - i0) * GROUP)
            found = lax.dot_general(
                members[0, js], members[0, iss], contract_last, preferred_element_type=jnp.float32
            )
            column = jnp.concatenate([rank_column[0, js]] * (i1 - i0), axis=1)
            row = rank_row[:, iss]
            down = jnp.max(
                jnp.where(column < row, found, -1.0).reshape((j1 - j0) * GROUP // 8, 8, (i1 - i0) * GROUP), axis=0
            )
            best[:, iss] = jnp.maximum(best[:, iss], down)
            across = jnp.where(row < column, found, -1.0)
            parts = [across[:, GROUP * n : GROUP * (n + 1)] for n in range(i1 - i0)]
            while len(parts) > 1:
                parts = [jnp.maximum(a, b) for a, b in zip(parts[::2], parts[1::2])] + parts[len(parts) // 2 * 2 :]
            turned_best[js] = jnp.maximum(turned_best[js], parts[0])

        def ranks(side):
            for t in range(GROUPS):
                row = jnp.sum(member_rank[side, t].reshape(4, GROUP), axis=0, keepdims=True)
                if side == 0:
                    rank_row[:, pl.ds(t * GROUP, GROUP)] = row
                rank_column[side, pl.ds(t * GROUP, GROUP)] = jnp.broadcast_to(row, (GROUP, GROUP)).T

        def part(k, side):
            return members.at[side, pl.ds(STARTS[k] * GROUP, STEPS[k] * GROUP)]

        arrived(member_rank.at[0], rank_sem)
        remote(member_rank.at[0], member_rank.at[1], pair_rank_send_sem, pair_rank_sem, sibling).start()
        ranks(0)
        arrived(member_rank.at[1], pair_rank_sem)
        ranks(1)

        last = len(STEPS)
        for k in range(last + 1):
            s, e = (STARTS[k], STARTS[k + 1]) if k < last else (GROUPS, GROUPS)
            if k < last:
                arrived(part(k, 0), member_sem.at[k])
                remote(part(k, 0), part(k, 1), pair_send_sem, pair_sem.at[k], sibling).start()
            if k > 0:
                p, q = STARTS[k - 1], STARTS[k]
                arrived(part(k - 1, 1), pair_sem.at[k - 1])
                scores(1, p, q, 0, e)
                scores(1, 0, p, s, e)
                if k == last:
                    for t in range(p):
                        lanes = pl.ds(t * GROUP, GROUP)
                        other = jnp.max(turned_best[lanes].T.reshape(GROUP // 8, 8, GROUP), axis=0)
                        best[:, lanes] = jnp.maximum(best[:, lanes], other)
            if k < last:
                both(0, s, s, e)
                scores(0, s, e, s, e)

        for t, (dx, dz) in enumerate(ORDER):
            reply[t] = jnp.max(best[:, pl.ds(t * GROUP, GROUP)], axis=0, keepdims=True)
            for sy in range(4):
                target = place((x + dx) % 4, sy, (z + turned(dz, z % 2)) % 4, core)

                def away():
                    remote(reply.at[t], back.at[own], back_send_sem, back_sem, target).start()

                if (dx, dz) == (0, 0):
                    pl.when(sy != y)(away)

                    @pl.when(sy == y)
                    def _():
                        pltpu.make_async_copy(reply.at[t], back.at[own], back_sem).start()
                else:
                    away()

    arrived(back, back_sem)
    table = back[...].reshape(CLUSTERS, GROUP)
    found = lax.dot_general(
        table, onehot, (((0,), (0,)), ((), ())),
        precision=lax.Precision.HIGHEST, preferred_element_type=jnp.float32,
    )
    out_ref[...] = jnp.sum(jnp.where(lane_hit, found, 0.0), axis=0, keepdims=True)

    @pl.when(holds)
    def _():
        arrived(outgoing.at[pl.ds(0, CLUSTERS - 1)], send_sem)
        arrived(out_rank.at[pl.ds(0, CLUSTERS - 1)], rank_send_sem)
        arrived(members.at[0], pair_send_sem)
        arrived(member_rank.at[0], pair_rank_send_sem)
        arrived(back, back_send_sem)
        arrived(back.at[pl.ds(0, CLUSTERS - 1)], back_send_sem)

    @pl.when(jnp.logical_not(holds))
    def _():
        arrived(outgoing, send_sem)
        arrived(out_rank, rank_send_sem)
        arrived(passing, pass_send_sem)


def body(embedding, cluster, rank):
    rows, width = embedding.shape
    vmem = pl.BlockSpec(memory_space=pltpu.VMEM)
    dma = pltpu.SemaphoreType.DMA
    steps = len(STEPS)
    found = pl.pallas_call(
        kernel,
        out_shape=jax.ShapeDtypeStruct((1, rows), jnp.float32),
        in_specs=[pl.BlockSpec(memory_space=pl.ANY)] * 3,
        out_specs=vmem,
        scratch_shapes=[
            pltpu.VMEM((rows, width), jnp.bfloat16),
            pltpu.VMEM((1, rows), jnp.int32),
            pltpu.VMEM((1, rows), jnp.int32),
            pltpu.VMEM((CLUSTERS, SLOTS, width), jnp.bfloat16),
            pltpu.VMEM((CLUSTERS, 1, GROUP), jnp.float32),
            pltpu.VMEM((len(RELAYED), 4, SLOTS, width), jnp.bfloat16),
            pltpu.VMEM((2, GROUPS * GROUP, width), jnp.bfloat16),
            pltpu.VMEM((2, GROUPS, 4, 1, GROUP), jnp.float32),
            pltpu.VMEM((2, GROUPS * GROUP, GROUP), jnp.float32),
            pltpu.VMEM((1, GROUPS * GROUP), jnp.float32),
            pltpu.VMEM((8, GROUPS * GROUP), jnp.float32),
            pltpu.VMEM((STARTS[-2] * GROUP, GROUP), jnp.float32),
            pltpu.VMEM((GROUPS, 1, GROUP), jnp.float32),
            pltpu.VMEM((CLUSTERS, 1, GROUP), jnp.float32),
            dma((3,)), dma, dma, dma((len(RELAYED), 4)), dma, dma((steps,)), dma,
            dma, dma, dma((steps,)), dma, dma, dma,
        ],
        compiler_params=pltpu.CompilerParams(
            collective_id=0, has_side_effects=True, vmem_limit_bytes=56 << 20
        ),
    )(embedding, cluster.reshape(1, rows), rank.reshape(1, rows))
    return found.reshape(rows)


def solution(mesh):
    return jax.shard_map(
        body,
        mesh=mesh,
        in_specs=(P(("shard", "split"), None), P(("shard", "split")), P(("shard", "split"))),
        out_specs=P(("shard", "split")),
        check_vma=False,
    )
```

```python
import jax
import jax.numpy as jnp
from jax import lax
from jax.experimental import pallas as pl
from jax.experimental.pallas import tpu as pltpu
from jax.sharding import PartitionSpec as P

MESH = pl.DeviceIdType.MESH
CLUSTERS = 32
SLOTS = 32
GROUP = 4 * SLOTS
GROUPS = 16
PARITY = 0
NO_RANK = float(1 << 30)
ORDER = [
    (0, 0), (1, 0), (3, 0), (2, 0), (0, 1), (1, 1), (3, 1), (2, 1),
    (1, 3), (3, 3), (0, 2), (1, 2), (3, 2), (2, 3), (2, 2), (0, 3),
]
RELAYED = {(2, 3): 3, (2, 2): 1, (0, 3): 3}
SENDS = list(RELAYED) + [d for d in ORDER[::-1] if d not in RELAYED]
STEPS = [8, 4, 4]
STARTS = [sum(STEPS[:k]) for k in range(len(STEPS) + 1)]


def place(x, y, z, core):
    return (2 * x + core, 4 * z + y)


def turned(dz, odd):
    return dz if dz % 2 == 0 else (dz + 2 * odd) % 4


def step_of(t):
    return max(k for k in range(len(STEPS)) if STARTS[k] <= t)


def arrived(ref, sem):
    pltpu.make_async_copy(ref, ref, sem).wait()


def remote(src, dst, send_sem, recv_sem, target):
    return pltpu.make_async_remote_copy(
        src, dst, send_sem, recv_sem, device_id=target, device_id_type=MESH
    )


def kernel(
    embedding_any, cluster_any, rank_any, out_ref,
    embedding_ref, cluster_ref, rank_ref, outgoing, out_rank, passing, members, member_rank, rank_column, rank_row, best, turned_best, reply, back,
    load_sem, send_sem, rank_send_sem, pass_sem, pass_send_sem, member_sem, rank_sem,
    pair_send_sem, pair_rank_send_sem, pair_sem, pair_rank_sem, back_send_sem, back_sem,
):
    shard, split = lax.axis_index("shard"), lax.axis_index("split")
    x, core, z, y = shard // 2, shard % 2, split // 4, split % 4
    holds = (x + y + z) % 2 == PARITY
    own = x + 4 * y + 16 * (z // 2)
    rows = embedding_ref.shape[0]
    loads = [
        pltpu.make_async_copy(src, dst, load_sem.at[n])
        for n, (src, dst) in enumerate(
            [(embedding_any, embedding_ref), (cluster_any, cluster_ref), (rank_any, rank_ref)]
        )
    ]
    for load in loads:
        load.start()

    barrier = pltpu.get_barrier_semaphore()

    def greet(gx, gy, gz, gcore):
        pl.semaphore_signal(barrier, inc=1, device_id=place(gx, gy, gz, gcore), device_id_type=MESH)

    @pl.when(holds)
    def _():
        for s in range(64):
            greet(s % 4, s // 4 % 4, s // 16, core)
        greet(x, y, z, 1 - core)

    @pl.when(jnp.logical_not(holds))
    def _():
        for (dx, dz), aside in RELAYED.items():
            for sy in range(4):
                greet((x + 4 - aside + dx) % 4, sy, (z + turned(dz, z % 2)) % 4, core)

    for load in loads:
        load.wait()
    values = embedding_ref[...].astype(jnp.float32)
    unit = (
        values * lax.rsqrt(jnp.sum(values * values, axis=1, keepdims=True) + 1e-06)
    ).astype(jnp.bfloat16)
    cluster = cluster_ref[...]
    rank = rank_ref[...]
    cluster_hit = lax.broadcasted_iota(jnp.int32, (CLUSTERS, rows), 0) == cluster
    onehot = cluster_hit.astype(jnp.float32)
    earlier = (
        lax.broadcasted_iota(jnp.int32, (rows, rows), 0) < lax.broadcasted_iota(jnp.int32, (rows, rows), 1)
    ).astype(jnp.float32).astype(jnp.bfloat16)
    before = jnp.dot(onehot.astype(jnp.bfloat16), earlier, preferred_element_type=jnp.float32)
    position = jnp.sum(before * onehot, axis=0, keepdims=True).astype(jnp.int32)
    slot = cluster * SLOTS + position

    for part in range(CLUSTERS * SLOTS // 256):
        pick = (
            lax.broadcasted_iota(jnp.int32, (256, rows), 0) + part * 256 == slot
        ).astype(jnp.float32).astype(jnp.bfloat16)
        packed = jnp.dot(pick, unit, preferred_element_type=jnp.float32).astype(jnp.bfloat16)
        outgoing[pl.ds(part * 8, 8)] = packed.reshape(8, SLOTS, packed.shape[1])

    lane_hit = lax.broadcasted_iota(jnp.int32, (GROUP, rows), 0) == position + SLOTS * y
    lane_onehot = lane_hit.astype(jnp.float32).astype(jnp.bfloat16)
    contract_last = (((1,), (1,)), ((), ()))

    def spread(part):
        return lax.dot_general(
            (onehot * part.astype(jnp.float32)).astype(jnp.bfloat16), lane_onehot, contract_last,
            preferred_element_type=jnp.float32,
        )

    taken = spread(jnp.ones_like(rank))
    slot_rank = (
        spread(rank % 128) + 128.0 * spread(rank // 128 % 128) + 16384.0 * spread(rank // 16384)
    )
    mine = lax.broadcasted_iota(jnp.int32, (CLUSTERS, GROUP), 1) // SLOTS == y
    out_rank[...] = jnp.where(mine, jnp.where(taken > 0.5, slot_rank, NO_RANK), 0.0).reshape(CLUSTERS, 1, GROUP)

    pl.semaphore_wait(barrier, CLUSTERS + 2 * len(RELAYED) + jnp.where(holds, 1, 0))

    for dx, dz in SENDS:
        ax, az = (x + 4 - dx) % 4, (z + 4 - turned(dz, (z + dz) % 2)) % 4
        for half in range(2):
            ay = (y + (ax + y + az + PARITY) % 2 + 2 * half) % 4
            c = ax + 4 * ay + 16 * (az // 2)
            there = member_rank.at[0, ORDER.index((dx, dz)), y]

            def away():
                remote(out_rank.at[c], there, rank_send_sem, rank_sem, place(ax, ay, az, core)).start()

            if (dx, dz) == (0, 0):
                pl.when(ay != y)(away)

                @pl.when(ay == y)
                def _():
                    pltpu.make_async_copy(out_rank.at[c], there, rank_sem).start()
            else:
                away()

    for dx, dz in SENDS:
        t = ORDER.index((dx, dz))
        ax, az = (x + 4 - dx) % 4, (z + 4 - turned(dz, (z + dz) % 2)) % 4
        for half in range(2):
            ay = (y + (ax + y + az + PARITY) % 2 + 2 * half) % 4
            c = ax + 4 * ay + 16 * (az // 2)
            if (dx, dz) in RELAYED:
                side = list(RELAYED).index((dx, dz))
                target = place((ax + RELAYED[dx, dz]) % 4, ay, az, core)
                remote(outgoing.at[c], passing.at[side, y], send_sem, pass_sem.at[side, y], target).start()
                continue
            k = step_of(t)
            there = members.at[0, pl.ds(pl.multiple_of(t * GROUP + y * SLOTS, SLOTS), SLOTS)]
            there_sem = member_sem.at[k]
            target = place(ax, ay, az, core)

            def away():
                remote(outgoing.at[c], there, send_sem, there_sem, target).start()

            if (dx, dz) == (0, 0):
                pl.when(ay != y)(away)

                @pl.when(ay == y)
                def _():
                    pltpu.make_async_copy(outgoing.at[c], there, there_sem).start()
            else:
                away()

    @pl.when(jnp.logical_not(holds))
    def _():
        for side, ((dx, dz), aside) in enumerate(RELAYED.items()):
            t = ORDER.index((dx, dz))
            target = place((x + 4 - aside) % 4, y, z, core)
            for sy in range(4):
                arrived(passing.at[side, sy], pass_sem.at[side, sy])
                remote(
                    passing.at[side, sy], members.at[0, pl.ds(t * GROUP + sy * SLOTS, SLOTS)], pass_send_sem,
                    member_sem.at[step_of(t)], target,
                ).start()

    @pl.when(holds)
    def _():
        best[...] = jnp.full(best.shape, -1.0, jnp.float32)
        turned_best[...] = jnp.full(turned_best.shape, -1.0, jnp.float32)
        sibling = place(x, y, z, 1 - core)

        def scores(side, j0, j1, i0, i1):
            if j0 == j1 or i0 == i1:
                return
            js, iss = pl.ds(j0 * GROUP, (j1 - j0) * GROUP), pl.ds(i0 * GROUP, (i1 - i0) * GROUP)
            found = lax.dot_general(
                members[side, js], members[0, iss], contract_last, preferred_element_type=jnp.float32
            )
            column = jnp.concatenate([rank_column[side, js]] * (i1 - i0), axis=1)
            found = jnp.where(column < rank_row[:, iss], found, -1.0)
            found = jnp.max(found.reshape((j1 - j0) * GROUP // 8, 8, (i1 - i0) * GROUP), axis=0)
            best[:, iss] = jnp.maximum(best[:, iss], found)

        def both(j0, j1, i0, i1):
            if j0 == j1 or i0 == i1:
                return
            js, iss = pl.ds(j0 * GROUP, (j1 - j0) * GROUP), pl.ds(i0 * GROUP, (i1 - i0) * GROUP)
            found = lax.dot_general(
                members[0, js], members[0, iss], contract_last, preferred_element_type=jnp.float32
            )
            column = jnp.concatenate([rank_column[0, js]] * (i1 - i0), axis=1)
            row = rank_row[:, iss]
            down = jnp.max(
                jnp.where(column < row, found, -1.0).reshape((j1 - j0) * GROUP // 8, 8, (i1 - i0) * GROUP), axis=0
            )
            best[:, iss] = jnp.maximum(best[:, iss], down)
            across = jnp.where(row < column, found, -1.0)
            parts = [across[:, GROUP * n : GROUP * (n + 1)] for n in range(i1 - i0)]
            while len(parts) > 1:
                parts = [jnp.maximum(a, b) for a, b in zip(parts[::2], parts[1::2])] + parts[len(parts) // 2 * 2 :]
            turned_best[js] = jnp.maximum(turned_best[js], parts[0])

        def ranks(side):
            for t in range(GROUPS):
                row = jnp.sum(member_rank[side, t].reshape(4, GROUP), axis=0, keepdims=True)
                if side == 0:
                    rank_row[:, pl.ds(t * GROUP, GROUP)] = row
                rank_column[side, pl.ds(t * GROUP, GROUP)] = jnp.broadcast_to(row, (GROUP, GROUP)).T

        def part(k, side):
            return members.at[side, pl.ds(STARTS[k] * GROUP, STEPS[k] * GROUP)]

        arrived(member_rank.at[0], rank_sem)
        remote(member_rank.at[0], member_rank.at[1], pair_rank_send_sem, pair_rank_sem, sibling).start()
        ranks(0)
        arrived(member_rank.at[1], pair_rank_sem)
        ranks(1)

        last = len(STEPS)
        for k in range(last + 1):
            s, e = (STARTS[k], STARTS[k + 1]) if k < last else (GROUPS, GROUPS)
            if k < last:
                arrived(part(k, 0), member_sem.at[k])
                remote(part(k, 0), part(k, 1), pair_send_sem, pair_sem.at[k], sibling).start()
            if k > 0:
                p, q = STARTS[k - 1], STARTS[k]
                arrived(part(k - 1, 1), pair_sem.at[k - 1])
                scores(1, p, q, 0, e)
                scores(1, 0, p, s, e)
                if k == last:
                    for t in range(p):
                        lanes = pl.ds(t * GROUP, GROUP)
                        other = jnp.max(turned_best[lanes].T.reshape(GROUP // 8, 8, GROUP), axis=0)
                        best[:, lanes] = jnp.maximum(best[:, lanes], other)
            if k < last:
                both(0, s, s, e)
                scores(0, s, e, s, e)

        for t, (dx, dz) in enumerate(ORDER):
            reply[t] = jnp.max(best[:, pl.ds(t * GROUP, GROUP)], axis=0, keepdims=True)
            for sy in range(4):
                target = place((x + dx) % 4, sy, (z + turned(dz, z % 2)) % 4, core)

                def away():
                    remote(reply.at[t], back.at[own], back_send_sem, back_sem, target).start()

                if (dx, dz) == (0, 0):
                    pl.when(sy != y)(away)

                    @pl.when(sy == y)
                    def _():
                        pltpu.make_async_copy(reply.at[t], back.at[own], back_sem).start()
                else:
                    away()

    arrived(back, back_sem)
    table = back[...].reshape(CLUSTERS, GROUP)
    high = table.astype(jnp.bfloat16)
    rest = table - high.astype(jnp.float32)
    middle = rest.astype(jnp.bfloat16)
    low = (rest - middle.astype(jnp.float32)).astype(jnp.bfloat16)
    found = lax.dot_general(
        jnp.concatenate([high, middle, low], axis=0), jnp.concatenate([onehot.astype(jnp.bfloat16)] * 3, axis=0),
        (((0,), (0,)), ((), ())), preferred_element_type=jnp.float32,
    )
    out_ref[...] = jnp.sum(jnp.where(lane_hit, found, 0.0), axis=0, keepdims=True)

    @pl.when(holds)
    def _():
        arrived(outgoing.at[pl.ds(0, CLUSTERS - 1)], send_sem)
        arrived(out_rank.at[pl.ds(0, CLUSTERS - 1)], rank_send_sem)
        arrived(members.at[0], pair_send_sem)
        arrived(member_rank.at[0], pair_rank_send_sem)
        arrived(back, back_send_sem)
        arrived(back.at[pl.ds(0, CLUSTERS - 1)], back_send_sem)

    @pl.when(jnp.logical_not(holds))
    def _():
        arrived(outgoing, send_sem)
        arrived(out_rank, rank_send_sem)
        arrived(passing, pass_send_sem)


def body(embedding, cluster, rank):
    rows, width = embedding.shape
    vmem = pl.BlockSpec(memory_space=pltpu.VMEM)
    dma = pltpu.SemaphoreType.DMA
    steps = len(STEPS)
    found = pl.pallas_call(
        kernel,
        out_shape=jax.ShapeDtypeStruct((1, rows), jnp.float32),
        in_specs=[pl.BlockSpec(memory_space=pl.ANY)] * 3,
        out_specs=vmem,
        scratch_shapes=[
            pltpu.VMEM((rows, width), jnp.bfloat16),
            pltpu.VMEM((1, rows), jnp.int32),
            pltpu.VMEM((1, rows), jnp.int32),
            pltpu.VMEM((CLUSTERS, SLOTS, width), jnp.bfloat16),
            pltpu.VMEM((CLUSTERS, 1, GROUP), jnp.float32),
            pltpu.VMEM((len(RELAYED), 4, SLOTS, width), jnp.bfloat16),
            pltpu.VMEM((2, GROUPS * GROUP, width), jnp.bfloat16),
            pltpu.VMEM((2, GROUPS, 4, 1, GROUP), jnp.float32),
            pltpu.VMEM((2, GROUPS * GROUP, GROUP), jnp.float32),
            pltpu.VMEM((1, GROUPS * GROUP), jnp.float32),
            pltpu.VMEM((8, GROUPS * GROUP), jnp.float32),
            pltpu.VMEM((STARTS[-2] * GROUP, GROUP), jnp.float32),
            pltpu.VMEM((GROUPS, 1, GROUP), jnp.float32),
            pltpu.VMEM((CLUSTERS, 1, GROUP), jnp.float32),
            dma((3,)), dma, dma, dma((len(RELAYED), 4)), dma, dma((steps,)), dma,
            dma, dma, dma((steps,)), dma, dma, dma,
        ],
        compiler_params=pltpu.CompilerParams(
            collective_id=0, has_side_effects=True, vmem_limit_bytes=56 << 20
        ),
    )(embedding, cluster.reshape(1, rows), rank.reshape(1, rows))
    return found.reshape(rows)


def solution(mesh):
    return jax.shard_map(
        body,
        mesh=mesh,
        in_specs=(P(("shard", "split"), None), P(("shard", "split")), P(("shard", "split"))),
        out_specs=P(("shard", "split")),
        check_vma=False,
    )
```
